1024 devices in a mesh: row: 32 (over z), col: 32 (over x, y, core).
Axes of the slice: x: 4, y: 4, z: 32, core: 2. Of those that a mesh axis runs over, the one named last changes fastest.
Arguments:
- features: bfloat16 [65536, 512], P(('col', 'row')), may hold values from -6 to 6
- block_index: int32 [32, 32, 16], P('row', 'col'), may hold values from 0 to 255, as said below
- block_count: int32 [32, 32], P('row', 'col'), may hold values from 4 to 16, as said below
- block_values: bfloat16 [32, 32, 16, 128, 128], P('row', 'col'), may hold values from -0.3125 to 0.3125
- weight: bfloat16 [512, 512], replicated, may hold values from -0.25 to 0.25
- bias: float32 [512], replicated, may hold values from -3 to 3
Outputs:
- activated: bfloat16 [65536, 512], P(('row', 'col'))
The draws below stay inside these ranges and needn't reach their ends.
Inputs may be any that keep to these rules, and one draw needn't show every extreme that they name: `block_index`: within one tile all 16 entries are distinct. `block_count`: some tile holds exactly 16 live slots.
All inputs are finite; a program needn't handle non-finite values.
Results may differ from the reference program's by a relative error of at most 0.02.
Values may be sent and summed in bfloat16 or wider, within the bound.
No kernel may reach another device: no remote copies, remote signals or barrier semaphores. Data moves between devices by JAX's collectives and lax.ppermute only.
A program may use at most 32 MiB of HBM per device.

```python
import jax
import jax.numpy as jnp
from jax import lax

NODE_DEV = 64
BLOCK = 128
FEAT = 512
WIDTH = 512
NODES = 65536
SLOTS = 16
N_ROW = 32
N_COL = 32


def draw_block_index(key, part):
    key = jax.random.fold_in(key, 11)
    places = NODE_DEV * N_COL // BLOCK * (NODE_DEV * N_ROW // BLOCK)
    scores = jax.random.randint(key, (N_ROW, N_COL, places), 0, 1 << 20) * places + jnp.arange(places, dtype=jnp.int32)
    order = jnp.argsort(scores, axis=-1, stable=True)
    return order[:, :, :SLOTS].astype(jnp.int32)


def draw_block_count(key, part):
    key = jax.random.fold_in(key, 23)
    first, second = jax.random.split(key)
    counts = jax.random.randint(first, (N_ROW * N_COL,), max(1, SLOTS // 4), SLOTS + 1)
    chosen = jax.random.randint(second, (), 0, N_ROW * N_COL)
    counts = counts.at[chosen].set(SLOTS)
    return counts.reshape(N_ROW, N_COL).astype(jnp.int32)


def shard_levels(key, dims, pieces, low, top_value):
    def one(dim, shards_of):
        draws = jax.random.uniform(jax.random.fold_in(jax.random.fold_in(key, 6), dim), (shards_of,), jnp.float32, low / len(pieces), top_value / len(pieces))
        return jnp.repeat(jnp.exp(draws), dims[dim] // shards_of).reshape((-1,) + (1,) * (len(dims) - dim - 1))

    loudness = one(*pieces[0])
    for cut in pieces[1:]:
        loudness = loudness * one(*cut)
    return loudness


def gaussian(stream_key, shape, scale, limit, cuts=(), kind=jnp.bfloat16):
    loudness = shard_levels(stream_key, shape, cuts, -0.22, 0.18) if cuts else 1.0
    drawn = jax.random.normal(stream_key, shape, jnp.float32) * scale * loudness
    return jnp.minimum(jnp.maximum(drawn, -limit), limit).astype(kind)


def setup_inputs(seed: int = 0) -> dict:
    splits = jax.random.split(jax.random.key(seed), 7)
    features = gaussian(splits[0], (NODES, FEAT), 1.0, 6.0, ((0, 1024),))
    block_index = draw_block_index(jax.random.fold_in(splits[6], 71), 0)
    block_count = draw_block_count(jax.random.fold_in(splits[6], 71), 0)
    block_values = gaussian(splits[3], (N_ROW, N_COL, SLOTS, BLOCK, BLOCK), ((5 * SLOTS * BLOCK * BLOCK // (8 * NODE_DEV)) ** -0.5), 0.3125, ((0, 32), (1, 32)))
    weight = gaussian(splits[4], (FEAT, WIDTH), FEAT ** -0.5, 0.25)
    bias = gaussian(splits[5], (WIDTH,), 0.5, 3.0, (), jnp.float32)
    return {"features": features, "block_index": block_index, "block_count": block_count, "block_values": block_values, "weight": weight, "bias": bias}


def reference(features, block_index, block_count, block_values, weight, bias):
    recv_nodes = NODE_DEV * N_COL
    send_nodes = NODE_DEV * N_ROW
    recv_blocks = recv_nodes // BLOCK
    send_blocks = send_nodes // BLOCK
    panels = features.reshape(N_COL, send_blocks, BLOCK, FEAT)
    slot_ids = jnp.arange(SLOTS, dtype=jnp.int32)
    row_ids = jnp.arange(recv_blocks, dtype=jnp.int32)

    def row_tile(tile_row):
        def step(total, tile_col):
            slot_index = block_index[tile_row, tile_col]
            live_count = block_count[tile_row, tile_col]
            tile_values = block_values[tile_row, tile_col].astype(jnp.float32)
            block_row = slot_index // send_blocks
            block_col = slot_index % send_blocks
            picked = panels[tile_col][block_col].astype(jnp.float32)
            products = jnp.einsum("bij,bjf->bif", tile_values, picked)
            select = ((block_row[None, :] == row_ids[:, None]) & (slot_ids[None, :] < live_count)).astype(jnp.float32)
            summed = jnp.einsum("rb,bif->rif", select, products, precision=lax.Precision.HIGHEST)
            rounded = lax.optimization_barrier(summed.astype(jnp.bfloat16))
            return total + rounded.astype(jnp.float32), None

        start = jnp.zeros((recv_blocks, BLOCK, FEAT), jnp.float32)
        total, _ = lax.scan(step, start, jnp.arange(N_COL, dtype=jnp.int32))
        return total

    tiles = lax.map(row_tile, jnp.arange(N_ROW, dtype=jnp.int32))
    aggregate = tiles.reshape(NODES, FEAT).astype(jnp.bfloat16)
    mixed = jnp.dot(aggregate, weight, preferred_element_type=jnp.float32) + bias
    return jax.nn.relu(mixed).astype(jnp.bfloat16)
```

```python
import functools

import jax
import jax.numpy as jnp
from jax import lax
from jax.experimental import pallas as pl
from jax.experimental.pallas import tpu as pltpu
from jax.sharding import Mesh, PartitionSpec as P

STRIDE = 4
Z = ("zo", "zi")
XY = ("x", "y")


def tile_kernel(
    index_ref, count_ref, values_ref, own_ref, below_ref, above_ref, low_ref, high_ref,
    mine_ref, theirs_ref, panel, total,
):
    place, core = lax.axis_index("zi"), lax.axis_index("core")
    slots, side = values_ref.shape[2], values_ref.shape[3]
    dests, shard, _ = mine_ref.shape
    send_blocks = panel.shape[0] // side

    def put(ref, step, first):
        start = lax.rem(place + step, STRIDE)
        for k in range(ref.shape[0] // shard):
            row = pl.multiple_of((start + STRIDE * (first + k)) * shard, shard)
            panel[pl.ds(row, shard), :] = ref[k * shard : (k + 1) * shard, :]

    put(own_ref, 0, 0)
    put(above_ref, 1, 0)
    put(low_ref, 2, 0)
    put(high_ref, 2, low_ref.shape[0] // shard)
    put(below_ref, STRIDE - 1, 0)
    total[...] = jnp.zeros_like(total)
    for s in range(slots):
        place_in_tile = index_ref[0, 0, s]
        block_row = place_in_tile // send_blocks
        block_col = place_in_tile % send_blocks

        @pl.when(s < count_ref[0, 0])
        def _():
            rows = pl.ds(pl.multiple_of(block_row * side, side), side)
            nodes = pl.ds(pl.multiple_of(block_col * side, side), side)
            total[rows, :] += jnp.dot(
                values_ref[0, 0, s], panel[nodes, :], preferred_element_type=jnp.float32
            )

    for d in range(dests):
        for ref, who in ((mine_ref, core), (theirs_ref, 1 - core)):
            row = pl.multiple_of((2 * d + who) * shard, shard)
            ref[d] = total[pl.ds(row, shard), :].astype(ref.dtype)


def final_kernel(parts_ref, weight_ref, bias_ref, out_ref):
    aggregate = jnp.sum(parts_ref[...].astype(jnp.float32), axis=0).astype(jnp.bfloat16)
    mixed = jnp.dot(aggregate, weight_ref[...], preferred_element_type=jnp.float32)
    out_ref[...] = jnp.maximum(mixed + bias_ref[...], 0.0).astype(out_ref.dtype)


def local(features, block_index, block_count, block_values, weight, bias):
    shard, feat = features.shape
    rows = lax.axis_size("zo")
    z_size = rows * STRIDE
    xy_size = lax.axis_size("x") * lax.axis_size("y")

    def shift(array, by):
        return lax.ppermute(array, Z, [(z, (z + by) % z_size) for z in range(z_size)])

    own = lax.all_gather(features, "zo", axis=0, tiled=True)
    half = own.shape[0] // 2
    low = shift(own[:half], 2)
    high = shift(own[half:], -2)
    below = shift(own, 1)
    above = shift(own, -1)

    smem = pl.BlockSpec(memory_space=pltpu.SMEM)
    vmem = pl.BlockSpec(memory_space=pltpu.VMEM)
    half_sums = jax.ShapeDtypeStruct((xy_size, shard, feat), jnp.bfloat16)
    slots, side = block_values.shape[2], block_values.shape[3]
    mine, theirs = pl.pallas_call(
        tile_kernel,
        out_shape=(half_sums, half_sums),
        in_specs=[smem, smem] + [vmem] * 6,
        out_specs=(vmem, vmem),
        scratch_shapes=[
            pltpu.VMEM((z_size * shard, feat), jnp.bfloat16),
            pltpu.VMEM((2 * xy_size * shard, feat), jnp.float32),
        ],
        compiler_params=pltpu.CompilerParams(vmem_limit_bytes=40 * 1024 * 1024),
        cost_estimate=pl.CostEstimate(
            flops=2 * slots * side * side * feat,
            bytes_accessed=slots * side * side * 2 + z_size * shard * feat * 4,
            transcendentals=0,
        ),
    )(block_index, block_count, block_values, own, below, above, low, high)

    sibling = lax.ppermute(theirs, "core", [(0, 1), (1, 0)])
    pair = (mine.astype(jnp.float32) + sibling.astype(jnp.float32)).astype(jnp.bfloat16)
    parts = lax.all_to_all(pair, XY, 0, 0, tiled=True)
    return pl.pallas_call(
        final_kernel,
        out_shape=jax.ShapeDtypeStruct((shard, weight.shape[1]), jnp.bfloat16),
        in_specs=[vmem] * 3,
        out_specs=vmem,
        compiler_params=pltpu.CompilerParams(vmem_limit_bytes=40 * 1024 * 1024),
    )(parts, weight, bias.reshape(1, -1))


def solution(mesh):
    z_size, col = mesh.devices.shape
    side = int(round((col // 2) ** 0.5))
    grid = Mesh(
        mesh.devices.reshape(z_size // STRIDE, STRIDE, side, col // 2 // side, 2),
        Z + XY + ("core",),
    )
    column = XY + ("core",)
    return jax.shard_map(
        local,
        mesh=grid,
        in_specs=(
            P(column + Z, None),
            P(Z, column, None),
            P(Z, column),
            P(Z, column, None, None, None),
            P(),
            P(),
        ),
        out_specs=P(Z + column, None),
        check_vma=False,
    )
```

```python
import functools

import jax
import jax.numpy as jnp
from jax import lax
from jax.experimental import pallas as pl
from jax.experimental.pallas import tpu as pltpu
from jax.sharding import Mesh, PartitionSpec as P

STRIDE = 4
Z = ("zo", "zi")
XY = ("x", "y")


def tile_kernel(
    index_ref, count_ref, values_ref, own_ref, below_ref, above_ref, far_ref,
    mine_ref, theirs_ref, panel, total,
):
    place, core = lax.axis_index("zi"), lax.axis_index("core")
    slots, side = values_ref.shape[2], values_ref.shape[3]
    dests, shard, _ = mine_ref.shape
    send_blocks = panel.shape[0] // side

    for step, ref in enumerate((own_ref, above_ref, far_ref, below_ref)):
        start = lax.rem(place + step, STRIDE)
        for k in range(ref.shape[0] // shard):
            row = pl.multiple_of((start + STRIDE * k) * shard, shard)
            panel[pl.ds(row, shard), :] = ref[k * shard : (k + 1) * shard, :]
    total[...] = jnp.zeros_like(total)
    for s in range(slots):
        place_in_tile = index_ref[0, 0, s]
        block_row = place_in_tile // send_blocks
        block_col = place_in_tile % send_blocks

        @pl.when(s < count_ref[0, 0])
        def _():
            rows = pl.ds(pl.multiple_of(block_row * side, side), side)
            nodes = pl.ds(pl.multiple_of(block_col * side, side), side)
            total[rows, :] += jnp.dot(
                values_ref[0, 0, s], panel[nodes, :], preferred_element_type=jnp.float32
            )

    for d in range(dests):
        for ref, who in ((mine_ref, core), (theirs_ref, 1 - core)):
            row = pl.multiple_of((2 * d + who) * shard, shard)
            ref[d] = total[pl.ds(row, shard), :].astype(ref.dtype)


def final_kernel(parts_ref, weight_ref, bias_ref, out_ref):
    aggregate = jnp.sum(parts_ref[...].astype(jnp.float32), axis=0).astype(jnp.bfloat16)
    mixed = jnp.dot(aggregate, weight_ref[...], preferred_element_type=jnp.float32)
    out_ref[...] = jnp.maximum(mixed + bias_ref[...], 0.0).astype(out_ref.dtype)


def local(features, block_index, block_count, block_values, weight, bias):
    shard, feat = features.shape
    rows = lax.axis_size("zo")
    z_size = rows * STRIDE
    xy_size = lax.axis_size("x") * lax.axis_size("y")

    def shift(array, by):
        return lax.ppermute(array, Z, [(z, (z + by) % z_size) for z in range(z_size)])

    own = lax.all_gather(features, "zo", axis=0, tiled=True)
    pairs = [(z, core) for z in range(z_size) for core in range(2)]
    far = lax.ppermute(
        own,
        Z + ("core",),
        [(2 * z + c, 2 * ((z - 2 + 4 * c) % z_size) + c) for z, c in pairs],
    )
    below = shift(own, 1)
    above = shift(own, -1)

    smem = pl.BlockSpec(memory_space=pltpu.SMEM)
    vmem = pl.BlockSpec(memory_space=pltpu.VMEM)
    half_sums = jax.ShapeDtypeStruct((xy_size, shard, feat), jnp.bfloat16)
    slots, side = block_values.shape[2], block_values.shape[3]
    mine, theirs = pl.pallas_call(
        tile_kernel,
        out_shape=(half_sums, half_sums),
        in_specs=[smem, smem] + [vmem] * 5,
        out_specs=(vmem, vmem),
        scratch_shapes=[
            pltpu.VMEM((z_size * shard, feat), jnp.bfloat16),
            pltpu.VMEM((2 * xy_size * shard, feat), jnp.float32),
        ],
        compiler_params=pltpu.CompilerParams(vmem_limit_bytes=40 * 1024 * 1024),
        cost_estimate=pl.CostEstimate(
            flops=2 * slots * side * side * feat,
            bytes_accessed=slots * side * side * 2 + z_size * shard * feat * 4,
            transcendentals=0,
        ),
    )(block_index, block_count, block_values, own, below, above, far)

    sibling = lax.ppermute(theirs, "core", [(0, 1), (1, 0)])
    pair = (mine.astype(jnp.float32) + sibling.astype(jnp.float32)).astype(jnp.bfloat16)
    parts = lax.all_to_all(pair, XY, 0, 0, tiled=True)
    return pl.pallas_call(
        final_kernel,
        out_shape=jax.ShapeDtypeStruct((shard, weight.shape[1]), jnp.bfloat16),
        in_specs=[vmem] * 3,
        out_specs=vmem,
        compiler_params=pltpu.CompilerParams(vmem_limit_bytes=40 * 1024 * 1024),
    )(parts, weight, bias.reshape(1, -1))


def solution(mesh):
    z_size, col = mesh.devices.shape
    side = int(round((col // 2) ** 0.5))
    grid = Mesh(
        mesh.devices.reshape(z_size // STRIDE, STRIDE, side, col // 2 // side, 2),
        Z + XY + ("core",),
    )
    column = XY + ("core",)
    return jax.shard_map(
        local,
        mesh=grid,
        in_specs=(
            P(column + Z, None),
            P(Z, column, None),
            P(Z, column),
            P(Z, column, None, None, None),
            P(),
            P(),
        ),
        out_specs=P(Z + column, None),
        check_vma=False,
    )
```

```python
import jax
import jax.numpy as jnp
from jax import lax
from jax.experimental import pallas as pl
from jax.experimental.pallas import tpu as pltpu
from jax.sharding import Mesh, PartitionSpec as P

STRIDE = 4
Z = ("zo", "zm", "zl")
XY = ("x", "y")


def tile_kernel(
    index_ref, count_ref, other_meta_ref, values_ref, other_values_ref,
    own_ref, above_ref, far_ref, below_ref, mine_ref, theirs_ref, panel, total,
):
    pair, core = lax.axis_index("zl"), lax.axis_index("core")
    place = 2 * lax.axis_index("zm") + pair
    slots, side = values_ref.shape[2], values_ref.shape[3]
    dests, shard, _ = mine_ref.shape
    dests = dests // 2
    send_blocks = panel.shape[0] // side

    for step, ref in enumerate((own_ref, above_ref, far_ref, below_ref)):
        start = lax.rem(place + step, STRIDE)
        for k in range(ref.shape[0] // shard):
            row = pl.multiple_of((start + STRIDE * k) * shard, shard)
            panel[pl.ds(row, shard), :] = ref[k * shard : (k + 1) * shard, :]

    def add_tile(values, place_of, count):
        total[...] = jnp.zeros_like(total)
        for s in range(slots):
            place_in_tile = place_of(s)
            block_row = place_in_tile // send_blocks
            block_col = place_in_tile % send_blocks

            @pl.when(s < count)
            def _():
                rows = pl.ds(pl.multiple_of(block_row * side, side), side)
                nodes = pl.ds(pl.multiple_of(block_col * side, side), side)
                total[rows, :] += jnp.dot(
                    values[0, 0, s], panel[nodes, :], preferred_element_type=jnp.float32
                )

    def store_tile(plane):
        for d in range(dests):
            for ref, who in ((mine_ref, core), (theirs_ref, 1 - core)):
                row = pl.multiple_of((2 * d + who) * shard, shard)
                ref[plane * dests + d] = total[pl.ds(row, shard), :].astype(ref.dtype)

    add_tile(values_ref, lambda s: index_ref[0, 0, s], count_ref[0, 0])
    store_tile(pair)
    add_tile(other_values_ref, lambda s: other_meta_ref[s], other_meta_ref[slots])
    store_tile(1 - pair)


def final_kernel(parts_ref, weight_ref, bias_ref, out_ref):
    half, width = parts_ref.shape[0] // 2, parts_ref.shape[2]
    mixed = bias_ref[...]
    for k in range(2):
        part = parts_ref[k * half : (k + 1) * half].astype(jnp.float32)
        aggregate = jnp.sum(part, axis=0).astype(jnp.bfloat16)
        mixed = mixed + jnp.dot(
            aggregate,
            weight_ref[k * width : (k + 1) * width, :],
            preferred_element_type=jnp.float32,
        )
    out_ref[...] = jnp.maximum(mixed, 0.0).astype(out_ref.dtype)


def local(features, block_index, block_count, block_values, weight, bias):
    shard, feat = features.shape
    width = feat // 2
    z_size = lax.axis_size("zo") * STRIDE
    xy_size = lax.axis_size("x") * lax.axis_size("y")
    pair = lax.axis_index("zl")

    def shift(array, by):
        return lax.ppermute(array, Z, [(z, (z + by) % z_size) for z in range(z_size)])

    def swap(array, axis):
        return lax.ppermute(array, axis, [(0, 1), (1, 0)])

    other_values = swap(block_values, "zl")
    own = lax.all_gather(features, "zo", axis=0, tiled=True)
    kept = lax.dynamic_slice_in_dim(own, pair * width, width, 1)
    given = lax.dynamic_slice_in_dim(own, (1 - pair) * width, width, 1)
    pairs = [(z, core) for z in range(z_size) for core in range(2)]
    far = lax.ppermute(
        kept,
        Z + ("core",),
        [(2 * z + c, 2 * ((z - 2 + 4 * c) % z_size) + c) for z, c in pairs],
    )
    below = shift(given, 1)
    above = shift(given, -1)
    meta = jnp.concatenate([block_index[0, 0], block_count[0]])
    meta, given = lax.optimization_barrier((meta, given))
    other_meta = swap(meta, "zl")

    smem = pl.BlockSpec(memory_space=pltpu.SMEM)
    vmem = pl.BlockSpec(memory_space=pltpu.VMEM)
    sums = jax.ShapeDtypeStruct((2 * xy_size, shard, width), jnp.bfloat16)
    slots, side = block_values.shape[2], block_values.shape[3]
    mine, theirs = pl.pallas_call(
        tile_kernel,
        out_shape=(sums, sums),
        in_specs=[smem] * 3 + [vmem] * 6,
        out_specs=(vmem, vmem),
        scratch_shapes=[
            pltpu.VMEM((z_size * shard, width), jnp.bfloat16),
            pltpu.VMEM((2 * xy_size * shard, width), jnp.float32),
        ],
        compiler_params=pltpu.CompilerParams(vmem_limit_bytes=24 * 1024 * 1024),
        cost_estimate=pl.CostEstimate(
            flops=2 * slots * side * side * feat,
            bytes_accessed=slots * side * side * 4 + z_size * shard * feat * 3,
            transcendentals=0,
        ),
    )(
        block_index, block_count, other_meta, block_values, other_values,
        kept, above, far, below,
    )

    sibling = swap(theirs, "core")
    both = (mine.astype(jnp.float32) + sibling.astype(jnp.float32)).astype(jnp.bfloat16)
    parts = lax.all_to_all(both, ("zl",) + XY, 0, 0, tiled=True)
    return pl.pallas_call(
        final_kernel,
        out_shape=jax.ShapeDtypeStruct((shard, weight.shape[1]), jnp.bfloat16),
        in_specs=[vmem] * 3,
        out_specs=vmem,
        compiler_params=pltpu.CompilerParams(vmem_limit_bytes=24 * 1024 * 1024),
    )(parts, weight, bias.reshape(1, -1))


def solution(mesh):
    z_size, col = mesh.devices.shape
    side = int(round((col // 2) ** 0.5))
    grid = Mesh(
        mesh.devices.reshape(z_size // STRIDE, STRIDE // 2, 2, side, col // 2 // side, 2),
        Z + XY + ("core",),
    )
    column = XY + ("core",)
    return jax.shard_map(
        local,
        mesh=grid,
        in_specs=(
            P(column + Z, None),
            P(Z, column, None),
            P(Z, column),
            P(Z, column, None, None, None),
            P(),
            P(),
        ),
        out_specs=P(Z + column, None),
        check_vma=False,
    )
```

```python
import jax
import jax.numpy as jnp
from jax import lax
from jax.experimental import pallas as pl
from jax.experimental.pallas import tpu as pltpu
from jax.sharding import Mesh, PartitionSpec as P

STRIDE = 4
Z = ("zo", "zi")
XY = ("x", "y")
VMEM_LIMIT = 16 * 1024 * 1024


def each_live(index_ref, count_ref, slots, send_blocks, work):
    for s in range(slots):
        place_in_tile = index_ref[0, 0, s]
        pl.when(s < count_ref[0, 0])(
            lambda s=s, e=place_in_tile: work(s, e // send_blocks, e % send_blocks)
        )


def near_kernel(
    index_ref, count_ref, values_ref, own_ref, first_ref, second_ref, total_ref, panel
):
    place, core = lax.axis_index("zi"), lax.axis_index("core")
    slots, side = values_ref.shape[2], values_ref.shape[3]
    shard = panel.shape[0] // lax.axis_size("zo") // STRIDE
    classes = lax.axis_size("zo")
    send_blocks = panel.shape[0] // side

    steps = (0, STRIDE - 1 - 2 * core, 1 + 2 * core, 2)
    for step, ref in zip(steps, (own_ref, first_ref, second_ref, None)):
        start = lax.rem(place + step, STRIDE)
        for k in range(classes):
            rows = pl.ds(pl.multiple_of((start + STRIDE * k) * shard, shard), shard)
            if ref is None:
                panel[rows, :] = jnp.zeros((shard, panel.shape[1]), panel.dtype)
            else:
                panel[rows, :] = ref[k * shard : (k + 1) * shard, :]
    total_ref[...] = jnp.zeros_like(total_ref)

    def work(s, block_row, block_col):
        rows = pl.ds(pl.multiple_of(block_row * side, side), side)
        nodes = pl.ds(pl.multiple_of(block_col * side, side), side)
        total_ref[rows, :] += jnp.dot(
            values_ref[0, 0, s], panel[nodes, :], preferred_element_type=jnp.float32
        )

    each_live(index_ref, count_ref, slots, send_blocks, work)


def far_kernel(
    index_ref, count_ref, values_ref, far_ref, total_in_ref, total_ref, theirs_ref
):
    del total_in_ref
    place, core = lax.axis_index("zi"), lax.axis_index("core")
    slots, side = values_ref.shape[2], values_ref.shape[3]
    dests, shard, _ = theirs_ref.shape
    send_blocks = far_ref.shape[0] * STRIDE // side
    far_class = lax.rem(place + 2, STRIDE)
    per_block = side // shard

    for part in range(per_block):

        def work(s, block_row, block_col, part=part):
            node = block_col * per_block + part

            @pl.when(lax.rem(node, STRIDE) == far_class)
            def _():
                rows = pl.ds(pl.multiple_of(block_row * side, side), side)
                nodes = pl.ds(pl.multiple_of(node // STRIDE * shard, shard), shard)
                total_ref[rows, :] += jnp.dot(
                    values_ref[0, 0, s, :, part * shard : (part + 1) * shard],
                    far_ref[nodes, :],
                    preferred_element_type=jnp.float32,
                )

        @pl.when(lax.rem(far_class, per_block) == part)
        def _():
            each_live(index_ref, count_ref, slots, send_blocks, work)

    for d in range(dests):
        row = pl.multiple_of((2 * d + 1 - core) * shard, shard)
        theirs_ref[d] = total_ref[pl.ds(row, shard), :].astype(theirs_ref.dtype)


def pair_kernel(total_ref, sibling_ref, out_ref):
    core = lax.axis_index("core")
    dests, shard, _ = out_ref.shape
    for d in range(dests):
        row = pl.multiple_of((2 * d + core) * shard, shard)
        mine = total_ref[pl.ds(row, shard), :]
        out_ref[d] = (mine + sibling_ref[d].astype(jnp.float32)).astype(out_ref.dtype)


def final_kernel(parts_ref, weight_ref, bias_ref, out_ref):
    aggregate = jnp.sum(parts_ref[...].astype(jnp.float32), axis=0).astype(jnp.bfloat16)
    mixed = jnp.dot(aggregate, weight_ref[...], preferred_element_type=jnp.float32)
    out_ref[...] = jnp.maximum(mixed + bias_ref[...], 0.0).astype(out_ref.dtype)


def local(features, block_index, block_count, block_values, weight, bias):
    shard, feat = features.shape
    rows = lax.axis_size("zo")
    z_size = rows * STRIDE
    xy_size = lax.axis_size("x") * lax.axis_size("y")

    def turn(array, sign):
        return lax.ppermute(
            array,
            Z + ("core",),
            [
                (2 * z + c, 2 * ((z + sign * (1 - 2 * c)) % z_size) + c)
                for z in range(z_size)
                for c in range(2)
            ],
        )

    own = lax.all_gather(features, "zo", axis=0, tiled=True)
    first = turn(own, 1)
    second = turn(own, -1)
    far = turn(first, 1)

    smem = pl.BlockSpec(memory_space=pltpu.SMEM)
    vmem = pl.BlockSpec(memory_space=pltpu.VMEM)
    params = pltpu.CompilerParams(vmem_limit_bytes=VMEM_LIMIT)
    rows_all = 2 * xy_size * shard
    sums = jax.ShapeDtypeStruct((rows_all, feat), jnp.float32)
    half_sums = jax.ShapeDtypeStruct((xy_size, shard, feat), jnp.bfloat16)
    slots, side = block_values.shape[2], block_values.shape[3]

    def cost(share):
        return pl.CostEstimate(
            flops=int(2 * slots * side * side * feat * share),
            bytes_accessed=int(rows_all * feat * 8 * share),
            transcendentals=0,
        )

    total = pl.pallas_call(
        near_kernel,
        out_shape=sums,
        in_specs=[smem, smem] + [vmem] * 4,
        out_specs=vmem,
        scratch_shapes=[pltpu.VMEM((z_size * shard, feat), jnp.bfloat16)],
        compiler_params=params,
        cost_estimate=cost(0.75),
    )(block_index, block_count, block_values, own, first, second)
    total, theirs = pl.pallas_call(
        far_kernel,
        out_shape=(sums, half_sums),
        in_specs=[smem, smem] + [vmem] * 3,
        out_specs=(vmem, vmem),
        input_output_aliases={4: 0},
        compiler_params=params,
        cost_estimate=cost(0.25),
    )(block_index, block_count, block_values, far, total)
    sibling = lax.ppermute(theirs, "core", [(0, 1), (1, 0)])
    both = pl.pallas_call(
        pair_kernel,
        out_shape=half_sums,
        in_specs=[vmem] * 2,
        out_specs=vmem,
        compiler_params=params,
    )(total, sibling)
    parts = lax.all_to_all(both, XY, 0, 0, tiled=True)
    return pl.pallas_call(
        final_kernel,
        out_shape=jax.ShapeDtypeStruct((shard, weight.shape[1]), jnp.bfloat16),
        in_specs=[vmem] * 3,
        out_specs=vmem,
        compiler_params=params,
    )(parts, weight, bias.reshape(1, -1))


def solution(mesh):
    z_size, col = mesh.devices.shape
    side = int(round((col // 2) ** 0.5))
    grid = Mesh(
        mesh.devices.reshape(z_size // STRIDE, STRIDE, side, col // 2 // side, 2),
        Z + XY + ("core",),
    )
    column = XY + ("core",)
    return jax.shard_map(
        local,
        mesh=grid,
        in_specs=(
            P(column + Z, None),
            P(Z, column, None),
            P(Z, column),
            P(Z, column, None, None, None),
            P(),
            P(),
        ),
        out_specs=P(Z + column, None),
        check_vma=False,
    )
```

```python
import jax
import jax.numpy as jnp
from jax import lax
from jax.experimental import pallas as pl
from jax.experimental.pallas import tpu as pltpu
from jax.sharding import Mesh, PartitionSpec as P

STRIDE = 4
Z = ("zo", "zi")
XY = ("x", "y")
VMEM_LIMIT = 16 * 1024 * 1024


def each_live(index_ref, count_ref, slots, send_blocks, work):
    for s in range(slots):
        place_in_tile = index_ref[0, 0, s]
        pl.when(s < count_ref[0, 0])(
            lambda s=s, e=place_in_tile: work(
                s, lax.div(e, send_blocks), lax.rem(e, send_blocks)
            )
        )


def near_kernel(
    index_ref, count_ref, values_ref, own_ref, first_low_ref, first_high_ref, second_ref,
    total_ref, panel,
):
    place, core = lax.axis_index("zi"), lax.axis_index("core")
    slots, side = values_ref.shape[2], values_ref.shape[3]
    shard = panel.shape[0] // lax.axis_size("zo") // STRIDE
    classes = lax.axis_size("zo")
    send_blocks = panel.shape[0] // side

    steps = (0, STRIDE - 1 - 2 * core, 1 + 2 * core, 2)
    sources = ((own_ref,), (first_low_ref, first_high_ref), (second_ref,), ())
    for step, refs in zip(steps, sources):
        start = lax.rem(place + step, STRIDE)
        shards = [r[k : k + shard, :] for r in refs for k in range(0, r.shape[0], shard)]
        for k in range(classes):
            rows = pl.ds(pl.multiple_of((start + STRIDE * k) * shard, shard), shard)
            if shards:
                panel[rows, :] = shards[k]
            else:
                panel[rows, :] = jnp.zeros((shard, panel.shape[1]), panel.dtype)
    total_ref[...] = jnp.zeros_like(total_ref)

    def work(s, block_row, block_col):
        rows = pl.ds(pl.multiple_of(block_row * side, side), side)
        nodes = pl.ds(pl.multiple_of(block_col * side, side), side)
        total_ref[rows, :] += jnp.dot(
            values_ref[0, 0, s], panel[nodes, :], preferred_element_type=jnp.float32
        )

    each_live(index_ref, count_ref, slots, send_blocks, work)


def far_kernel(
    index_ref, count_ref, values_ref, far_low_ref, far_high_ref, total_in_ref,
    total_ref, theirs_ref, far,
):
    del total_in_ref
    place, core = lax.axis_index("zi"), lax.axis_index("core")
    slots, side = values_ref.shape[2], values_ref.shape[3]
    dests, shard, _ = theirs_ref.shape
    send_blocks = far.shape[0] * STRIDE // side
    half = far_low_ref.shape[0]
    far[:half, :] = far_low_ref[...]
    far[half:, :] = far_high_ref[...]
    far_class = lax.rem(place + 2, STRIDE)
    per_block = side // shard

    for part in range(per_block):

        def work(s, block_row, block_col, part=part):
            node = block_col * per_block + part

            @pl.when(lax.rem(node, STRIDE) == far_class)
            def _():
                rows = pl.ds(pl.multiple_of(block_row * side, side), side)
                nodes = pl.ds(pl.multiple_of(lax.div(node, STRIDE) * shard, shard), shard)
                total_ref[rows, :] += jnp.dot(
                    values_ref[0, 0, s, :, part * shard : (part + 1) * shard],
                    far[nodes, :],
                    preferred_element_type=jnp.float32,
                )

        @pl.when(lax.rem(far_class, per_block) == part)
        def _():
            each_live(index_ref, count_ref, slots, send_blocks, work)

    for d in range(dests):
        row = pl.multiple_of((2 * d + 1 - core) * shard, shard)
        theirs_ref[d] = total_ref[pl.ds(row, shard), :].astype(theirs_ref.dtype)


def pair_kernel(total_ref, sibling_ref, out_ref):
    core = lax.axis_index("core")
    dests, shard, _ = out_ref.shape
    for d in range(dests):
        row = pl.multiple_of((2 * d + core) * shard, shard)
        mine = total_ref[pl.ds(row, shard), :]
        out_ref[d] = (mine + sibling_ref[d].astype(jnp.float32)).astype(out_ref.dtype)


def final_kernel(parts_ref, weight_ref, bias_ref, out_ref):
    aggregate = jnp.sum(parts_ref[...].astype(jnp.float32), axis=0).astype(jnp.bfloat16)
    mixed = jnp.dot(aggregate, weight_ref[...], preferred_element_type=jnp.float32)
    out_ref[...] = jnp.maximum(mixed + bias_ref[...], 0.0).astype(out_ref.dtype)


def local(features, block_index, block_count, block_values, weight, bias):
    shard, feat = features.shape
    rows = lax.axis_size("zo")
    z_size = rows * STRIDE
    xy_size = lax.axis_size("x") * lax.axis_size("y")

    def turn(array, sign):
        return lax.ppermute(
            array,
            Z + ("core",),
            [
                (2 * z + c, 2 * ((z + sign * (1 - 2 * c)) % z_size) + c)
                for z in range(z_size)
                for c in range(2)
            ],
        )

    own = lax.all_gather(features, "zo", axis=0, tiled=True)
    cut = (lax.axis_size("zo") * 5 // 8) * shard
    first = [turn(own[:cut], 1), turn(own[cut:], 1)]
    second = turn(own, -1)
    far = [turn(part, 1) for part in first]

    smem = pl.BlockSpec(memory_space=pltpu.SMEM)
    vmem = pl.BlockSpec(memory_space=pltpu.VMEM)
    params = pltpu.CompilerParams(vmem_limit_bytes=VMEM_LIMIT)
    rows_all = 2 * xy_size * shard
    sums = jax.ShapeDtypeStruct((rows_all, feat), jnp.float32)
    half_sums = jax.ShapeDtypeStruct((xy_size, shard, feat), jnp.bfloat16)
    slots, side = block_values.shape[2], block_values.shape[3]

    def cost(share):
        return pl.CostEstimate(
            flops=int(2 * slots * side * side * feat * share),
            bytes_accessed=int(rows_all * feat * 8 * share),
            transcendentals=0,
        )

    total = pl.pallas_call(
        near_kernel,
        out_shape=sums,
        in_specs=[smem, smem] + [vmem] * 5,
        out_specs=vmem,
        scratch_shapes=[pltpu.VMEM((z_size * shard, feat), jnp.bfloat16)],
        compiler_params=params,
        cost_estimate=cost(0.75),
    )(block_index, block_count, block_values, own, *first, second)
    total, theirs = pl.pallas_call(
        far_kernel,
        out_shape=(sums, half_sums),
        in_specs=[smem, smem] + [vmem] * 4,
        out_specs=(vmem, vmem),
        input_output_aliases={5: 0},
        scratch_shapes=[pltpu.VMEM(own.shape, own.dtype)],
        compiler_params=params,
        cost_estimate=cost(0.25),
    )(block_index, block_count, block_values, *far, total)
    sibling = lax.ppermute(theirs, "core", [(0, 1), (1, 0)])
    both = pl.pallas_call(
        pair_kernel,
        out_shape=half_sums,
        in_specs=[vmem] * 2,
        out_specs=vmem,
        compiler_params=params,
    )(total, sibling)
    parts = lax.all_to_all(both, XY, 0, 0, tiled=True)
    return pl.pallas_call(
        final_kernel,
        out_shape=jax.ShapeDtypeStruct((shard, weight.shape[1]), jnp.bfloat16),
        in_specs=[vmem] * 3,
        out_specs=vmem,
        compiler_params=params,
    )(parts, weight, bias.reshape(1, -1))


def solution(mesh):
    z_size, col = mesh.devices.shape
    side = int(round((col // 2) ** 0.5))
    grid = Mesh(
        mesh.devices.reshape(z_size // STRIDE, STRIDE, side, col // 2 // side, 2),
        Z + XY + ("core",),
    )
    column = XY + ("core",)
    return jax.shard_map(
        local,
        mesh=grid,
        in_specs=(
            P(column + Z, None),
            P(Z, column, None),
            P(Z, column),
            P(Z, column, None, None, None),
            P(),
            P(),
        ),
        out_specs=P(Z + column, None),
        check_vma=False,
    )
```

```python
import jax
import jax.numpy as jnp
from jax import lax
from jax.experimental import pallas as pl
from jax.experimental.pallas import tpu as pltpu
from jax.sharding import Mesh, PartitionSpec as P

STRIDE = 4
Z = ("zo", "zi")
XY = ("x", "y")
VMEM_LIMIT = 16 * 1024 * 1024


def each_slot(places, count, slots, send_blocks, work):
    for s in range(slots):
        place_in_tile = places(s)
        pl.when(s < count)(
            lambda s=s, e=place_in_tile: work(
                s, lax.div(e, send_blocks), lax.rem(e, send_blocks)
            )
        )


def near_kernel(
    count_ref, values_ref, index_ref, own_ref, first_low_ref, first_high_ref, second_ref,
    total_ref, kept_ref, places, panel, values_sem, index_sem,
):
    fetches = (
        pltpu.make_async_copy(values_ref, kept_ref, values_sem),
        pltpu.make_async_copy(index_ref, places, index_sem),
    )
    for fetch in fetches:
        fetch.start()
    place, core = lax.axis_index("zi"), lax.axis_index("core")
    slots, side = kept_ref.shape[2], kept_ref.shape[3]
    shard = panel.shape[0] // lax.axis_size("zo") // STRIDE
    classes = lax.axis_size("zo")
    send_blocks = panel.shape[0] // side

    steps = (0, STRIDE - 1 - 2 * core, 1 + 2 * core, 2)
    sources = ((own_ref,), (first_low_ref, first_high_ref), (second_ref,), ())
    for step, refs in zip(steps, sources):
        start = lax.rem(place + step, STRIDE)
        shards = [r[k : k + shard, :] for r in refs for k in range(0, r.shape[0], shard)]
        for k in range(classes):
            rows = pl.ds(pl.multiple_of((start + STRIDE * k) * shard, shard), shard)
            if shards:
                panel[rows, :] = shards[k]
            else:
                panel[rows, :] = jnp.zeros((shard, panel.shape[1]), panel.dtype)
    total_ref[...] = jnp.zeros_like(total_ref)
    for fetch in fetches:
        fetch.wait()

    def work(s, block_row, block_col):
        rows = pl.ds(pl.multiple_of(block_row * side, side), side)
        nodes = pl.ds(pl.multiple_of(block_col * side, side), side)
        total_ref[rows, :] += jnp.dot(
            kept_ref[0, 0, s], panel[nodes, :], preferred_element_type=jnp.float32
        )

    each_slot(lambda s: places[0, 0, s], count_ref[0, 0], slots, send_blocks, work)


def far_kernel(
    values_ref, index_ref, count_ref, far_low_ref, far_high_ref, total_in_ref,
    total_ref, theirs_ref, far,
):
    del total_in_ref
    place, core = lax.axis_index("zi"), lax.axis_index("core")
    slots, side = values_ref.shape[2], values_ref.shape[3]
    dests, shard, _ = theirs_ref.shape
    send_blocks = far.shape[0] * STRIDE // side
    half = far_low_ref.shape[0]
    far[:half, :] = far_low_ref[...]
    far[half:, :] = far_high_ref[...]
    far_class = lax.rem(place + 2, STRIDE)
    per_block = side // shard

    for part in range(per_block):

        def work(s, block_row, block_col, part=part):
            node = block_col * per_block + part

            @pl.when(lax.rem(node, STRIDE) == far_class)
            def _():
                rows = pl.ds(pl.multiple_of(block_row * side, side), side)
                nodes = pl.ds(pl.multiple_of(lax.div(node, STRIDE) * shard, shard), shard)
                total_ref[rows, :] += jnp.dot(
                    values_ref[0, 0, s, :, part * shard : (part + 1) * shard],
                    far[nodes, :],
                    preferred_element_type=jnp.float32,
                )

        @pl.when(lax.rem(far_class, per_block) == part)
        def _():
            each_slot(
                lambda s: index_ref[0, 0, s], count_ref[0, 0], slots, send_blocks, work
            )

    for d in range(dests):
        row = pl.multiple_of((2 * d + 1 - core) * shard, shard)
        theirs_ref[d] = total_ref[pl.ds(row, shard), :].astype(theirs_ref.dtype)


def pair_kernel(total_ref, sibling_ref, out_ref):
    core = lax.axis_index("core")
    dests, shard, _ = out_ref.shape
    for d in range(dests):
        row = pl.multiple_of((2 * d + core) * shard, shard)
        mine = total_ref[pl.ds(row, shard), :]
        out_ref[d] = (mine + sibling_ref[d].astype(jnp.float32)).astype(out_ref.dtype)


def final_kernel(parts_ref, weight_ref, bias_ref, out_ref):
    aggregate = jnp.sum(parts_ref[...].astype(jnp.float32), axis=0).astype(jnp.bfloat16)
    mixed = jnp.dot(aggregate, weight_ref[...], preferred_element_type=jnp.float32)
    out_ref[...] = jnp.maximum(mixed + bias_ref[...], 0.0).astype(out_ref.dtype)


def local(features, block_index, block_count, block_values, weight, bias):
    shard, feat = features.shape
    rows = lax.axis_size("zo")
    z_size = rows * STRIDE
    xy_size = lax.axis_size("x") * lax.axis_size("y")

    def turn(array, sign):
        return lax.ppermute(
            array,
            Z + ("core",),
            [
                (2 * z + c, 2 * ((z + sign * (1 - 2 * c)) % z_size) + c)
                for z in range(z_size)
                for c in range(2)
            ],
        )

    own = lax.all_gather(features, "zo", axis=0, tiled=True)
    cut = (lax.axis_size("zo") * 5 // 8) * shard
    first = [turn(own[:cut], 1), turn(own[cut:], 1)]
    second = turn(own, -1)
    far = [turn(part, 1) for part in first]

    smem = pl.BlockSpec(memory_space=pltpu.SMEM)
    vmem = pl.BlockSpec(memory_space=pltpu.VMEM)
    params = pltpu.CompilerParams(vmem_limit_bytes=VMEM_LIMIT)
    rows_all = 2 * xy_size * shard
    sums = jax.ShapeDtypeStruct((rows_all, feat), jnp.float32)
    half_sums = jax.ShapeDtypeStruct((xy_size, shard, feat), jnp.bfloat16)
    slots, side = block_values.shape[2], block_values.shape[3]

    def cost(share):
        return pl.CostEstimate(
            flops=int(2 * slots * side * side * feat * share),
            bytes_accessed=int(rows_all * feat * 8 * share),
            transcendentals=0,
        )

    tile = (block_values, block_index)
    total, *kept = pl.pallas_call(
        near_kernel,
        out_shape=(
            sums,
            *(jax.ShapeDtypeStruct(a.shape, a.dtype) for a in tile),
        ),
        in_specs=[smem] + [pl.BlockSpec(memory_space=pltpu.HBM)] * 2 + [vmem] * 4,
        out_specs=(vmem, vmem, smem),
        scratch_shapes=[
            pltpu.VMEM((z_size * shard, feat), jnp.bfloat16),
            pltpu.SemaphoreType.DMA,
            pltpu.SemaphoreType.DMA,
        ],
        compiler_params=params,
        cost_estimate=cost(0.75),
    )(
        block_count,
        *(pltpu.with_memory_space_constraint(array, pltpu.HBM) for array in tile),
        own,
        *first,
        second,
    )
    total, theirs = pl.pallas_call(
        far_kernel,
        out_shape=(sums, half_sums),
        in_specs=[vmem, smem, smem] + [vmem] * 3,
        out_specs=(vmem, vmem),
        input_output_aliases={5: 0},
        scratch_shapes=[pltpu.VMEM(own.shape, own.dtype)],
        compiler_params=params,
        cost_estimate=cost(0.25),
    )(*kept, block_count, *far, total)
    sibling = lax.ppermute(theirs, "core", [(0, 1), (1, 0)])
    both = pl.pallas_call(
        pair_kernel,
        out_shape=half_sums,
        in_specs=[vmem] * 2,
        out_specs=vmem,
        compiler_params=params,
    )(total, sibling)
    parts = lax.all_to_all(both, XY, 0, 0, tiled=True)
    return pl.pallas_call(
        final_kernel,
        out_shape=jax.ShapeDtypeStruct((shard, weight.shape[1]), jnp.bfloat16),
        in_specs=[vmem] * 3,
        out_specs=vmem,
        compiler_params=params,
    )(parts, weight, bias.reshape(1, -1))


def solution(mesh):
    z_size, col = mesh.devices.shape
    side = int(round((col // 2) ** 0.5))
    grid = Mesh(
        mesh.devices.reshape(z_size // STRIDE, STRIDE, side, col // 2 // side, 2),
        Z + XY + ("core",),
    )
    column = XY + ("core",)
    return jax.shard_map(
        local,
        mesh=grid,
        in_specs=(
            P(column + Z, None),
            P(Z, column, None),
            P(Z, column),
            P(Z, column, None, None, None),
            P(),
            P(),
        ),
        out_specs=P(Z + column, None),
        check_vma=False,
    )
```

```python
import jax
import jax.numpy as jnp
from jax import lax
from jax.experimental import pallas as pl
from jax.experimental.pallas import tpu as pltpu
from jax.sharding import Mesh, PartitionSpec as P

STRIDE = 4
Z = ("zo", "zi")
XY = ("x", "y")
VMEM_LIMIT = 16 * 1024 * 1024


def each_slot(places, count, slots, send_blocks, work):
    for s in range(slots):
        e = places(s)
        work(s, lax.div(e, send_blocks), lax.rem(e, send_blocks), s < count)


def near_kernel(
    count_ref, values_ref, index_ref, own_ref, first_low_ref, first_high_ref, second_ref,
    total_ref, kept_ref, places, panel, values_sem, index_sem,
):
    fetches = (
        pltpu.make_async_copy(values_ref, kept_ref, values_sem),
        pltpu.make_async_copy(index_ref, places, index_sem),
    )
    for fetch in fetches:
        fetch.start()
    place, core = lax.axis_index("zi"), lax.axis_index("core")
    slots, side = kept_ref.shape[2], kept_ref.shape[3]
    shard = panel.shape[0] // lax.axis_size("zo") // STRIDE
    classes = lax.axis_size("zo")
    send_blocks = panel.shape[0] // side

    steps = (0, STRIDE - 1 - 2 * core, 1 + 2 * core, 2)
    sources = ((own_ref,), (first_low_ref, first_high_ref), (second_ref,), ())
    for step, refs in zip(steps, sources):
        start = lax.rem(place + step, STRIDE)
        shards = [r[k : k + shard, :] for r in refs for k in range(0, r.shape[0], shard)]
        for k in range(classes):
            rows = pl.ds(pl.multiple_of((start + STRIDE * k) * shard, shard), shard)
            if shards:
                panel[rows, :] = shards[k]
            else:
                panel[rows, :] = jnp.zeros((shard, panel.shape[1]), panel.dtype)
    total_ref[...] = jnp.zeros_like(total_ref)
    for fetch in fetches:
        fetch.wait()

    def work(s, block_row, block_col, live):
        rows = pl.ds(pl.multiple_of(block_row * side, side), side)
        nodes = pl.ds(pl.multiple_of(block_col * side, side), side)
        values = jnp.where(live, kept_ref[0, 0, s], 0)
        total_ref[rows, :] += jnp.dot(
            values, panel[nodes, :], preferred_element_type=jnp.float32
        )

    each_slot(lambda s: places[0, 0, s], count_ref[0, 0], slots, send_blocks, work)


def far_kernel(
    values_ref, index_ref, count_ref, far_low_ref, far_high_ref, total_ref,
    total_out_ref, theirs_ref, mine_ref, far,
):
    del total_out_ref
    place, core = lax.axis_index("zi"), lax.axis_index("core")
    slots, side = values_ref.shape[2], values_ref.shape[3]
    dests, shard, _ = theirs_ref.shape
    send_blocks = far.shape[0] * STRIDE // side
    half = far_low_ref.shape[0]
    far[:half, :] = far_low_ref[...]
    far[half:, :] = far_high_ref[...]
    far_class = lax.rem(place + 2, STRIDE)
    per_block = side // shard

    for part in range(per_block):

        def work(s, block_row, block_col, live, part=part):
            node = block_col * per_block + part
            match = live & (lax.rem(node, STRIDE) == far_class)
            rows = pl.ds(pl.multiple_of(block_row * side, side), side)
            nodes = pl.ds(pl.multiple_of(lax.div(node, STRIDE) * shard, shard), shard)
            values = values_ref[0, 0, s, :, part * shard : (part + 1) * shard]
            total_ref[rows, :] += jnp.dot(
                jnp.where(match, values, 0),
                far[nodes, :],
                preferred_element_type=jnp.float32,
            )

        @pl.when(lax.rem(far_class, per_block) == part)
        def _():
            each_slot(
                lambda s: index_ref[0, 0, s], count_ref[0, 0], slots, send_blocks, work
            )

    for ref, who in ((theirs_ref, 1 - core), (mine_ref, core)):
        for d in range(dests):
            row = pl.multiple_of((2 * d + who) * shard, shard)
            ref[d] = total_ref[pl.ds(row, shard), :].astype(ref.dtype)


def pair_kernel(mine_ref, sibling_ref, out_ref):
    both = mine_ref[...] + sibling_ref[...].astype(jnp.float32)
    out_ref[...] = both.astype(out_ref.dtype)


def final_kernel(parts_ref, weight_ref, bias_ref, out_ref):
    aggregate = jnp.sum(parts_ref[...].astype(jnp.float32), axis=0).astype(jnp.bfloat16)
    mixed = jnp.dot(aggregate, weight_ref[...], preferred_element_type=jnp.float32)
    out_ref[...] = jnp.maximum(mixed + bias_ref[...], 0.0).astype(out_ref.dtype)


def local(features, block_index, block_count, block_values, weight, bias):
    shard, feat = features.shape
    rows = lax.axis_size("zo")
    z_size = rows * STRIDE
    xy_size = lax.axis_size("x") * lax.axis_size("y")

    def turn(array, sign):
        return lax.ppermute(
            array,
            Z + ("core",),
            [
                (2 * z + c, 2 * ((z + sign * (1 - 2 * c)) % z_size) + c)
                for z in range(z_size)
                for c in range(2)
            ],
        )

    own = lax.all_gather(features, "zo", axis=0, tiled=True)
    cut = (lax.axis_size("zo") * 5 // 8) * shard
    first = [turn(own[:cut], 1), turn(own[cut:], 1)]
    second = turn(own, -1)
    far = [turn(part, 1) for part in first]

    smem = pl.BlockSpec(memory_space=pltpu.SMEM)
    vmem = pl.BlockSpec(memory_space=pltpu.VMEM)
    params = pltpu.CompilerParams(vmem_limit_bytes=VMEM_LIMIT)
    rows_all = 2 * xy_size * shard
    sums = jax.ShapeDtypeStruct((rows_all, feat), jnp.float32)
    half_sums = jax.ShapeDtypeStruct((xy_size, shard, feat), jnp.bfloat16)
    slots, side = block_values.shape[2], block_values.shape[3]

    def cost(share):
        return pl.CostEstimate(
            flops=int(2 * slots * side * side * feat * share),
            bytes_accessed=int(rows_all * feat * 8 * share),
            transcendentals=0,
        )

    tile = (block_values, block_index)
    total, *kept = pl.pallas_call(
        near_kernel,
        out_shape=(
            sums,
            *(jax.ShapeDtypeStruct(a.shape, a.dtype) for a in tile),
        ),
        in_specs=[smem] + [pl.BlockSpec(memory_space=pltpu.HBM)] * 2 + [vmem] * 4,
        out_specs=(vmem, vmem, smem),
        scratch_shapes=[
            pltpu.VMEM((z_size * shard, feat), jnp.bfloat16),
            pltpu.SemaphoreType.DMA,
            pltpu.SemaphoreType.DMA,
        ],
        compiler_params=params,
        cost_estimate=cost(0.75),
    )(
        block_count,
        *(pltpu.with_memory_space_constraint(array, pltpu.HBM) for array in tile),
        own,
        *first,
        second,
    )
    _, theirs, mine = pl.pallas_call(
        far_kernel,
        out_shape=(sums, half_sums, jax.ShapeDtypeStruct(half_sums.shape, jnp.float32)),
        in_specs=[vmem, smem, smem] + [vmem] * 3,
        out_specs=(vmem, vmem, vmem),
        input_output_aliases={5: 0},
        scratch_shapes=[pltpu.VMEM(own.shape, own.dtype)],
        compiler_params=params,
        cost_estimate=cost(0.25),
    )(*kept, block_count, *far, total)
    sibling = lax.ppermute(theirs, "core", [(0, 1), (1, 0)])
    both = pl.pallas_call(
        pair_kernel,
        out_shape=half_sums,
        in_specs=[vmem] * 2,
        out_specs=vmem,
        compiler_params=params,
    )(mine, sibling)
    parts = lax.all_to_all(both, XY, 0, 0, tiled=True)
    return pl.pallas_call(
        final_kernel,
        out_shape=jax.ShapeDtypeStruct((shard, weight.shape[1]), jnp.bfloat16),
        in_specs=[vmem] * 3,
        out_specs=vmem,
        compiler_params=params,
    )(parts, weight, bias.reshape(1, -1))


def solution(mesh):
    z_size, col = mesh.devices.shape
    side = int(round((col // 2) ** 0.5))
    grid = Mesh(
        mesh.devices.reshape(z_size // STRIDE, STRIDE, side, col // 2 // side, 2),
        Z + XY + ("core",),
    )
    column = XY + ("core",)
    return jax.shard_map(
        local,
        mesh=grid,
        in_specs=(
            P(column + Z, None),
            P(Z, column, None),
            P(Z, column),
            P(Z, column, None, None, None),
            P(),
            P(),
        ),
        out_specs=P(Z + column, None),
        check_vma=False,
    )
```

```python
import jax
import jax.numpy as jnp
from jax import lax
from jax.experimental import pallas as pl
from jax.experimental.pallas import tpu as pltpu
from jax.sharding import Mesh, PartitionSpec as P

STRIDE = 4
Z = ("zo", "zi")
XY = ("x", "y")
VMEM_LIMIT = 16 * 1024 * 1024


def each_slot(places, count, slots, send_blocks, work):
    for s in range(slots):
        e = places(s)
        work(s, lax.div(e, send_blocks), lax.rem(e, send_blocks), s < count)


def near_kernel(
    count_ref, values_ref, index_ref, own_ref, first_low_ref, first_high_ref,
    total_ref, kept_ref, places, panel, values_sem, index_sem,
):
    fetches = (
        pltpu.make_async_copy(values_ref, kept_ref, values_sem),
        pltpu.make_async_copy(index_ref, places, index_sem),
    )
    for fetch in fetches:
        fetch.start()
    place, core = lax.axis_index("zi"), lax.axis_index("core")
    slots, side = kept_ref.shape[2], kept_ref.shape[3]
    shard = panel.shape[0] // lax.axis_size("zo") // STRIDE
    classes = lax.axis_size("zo")
    send_blocks = panel.shape[0] // side

    steps = (0, STRIDE - 1 - 2 * core, 1 + 2 * core, 2)
    sources = ((own_ref,), (first_low_ref, first_high_ref), (), ())
    for step, refs in zip(steps, sources):
        start = lax.rem(place + step, STRIDE)
        shards = [r[k : k + shard, :] for r in refs for k in range(0, r.shape[0], shard)]
        for k in range(classes):
            rows = pl.ds(pl.multiple_of((start + STRIDE * k) * shard, shard), shard)
            if shards:
                panel[rows, :] = shards[k]
            else:
                panel[rows, :] = jnp.zeros((shard, panel.shape[1]), panel.dtype)
    total_ref[...] = jnp.zeros_like(total_ref)
    for fetch in fetches:
        fetch.wait()

    def work(s, block_row, block_col, live):
        rows = pl.ds(pl.multiple_of(block_row * side, side), side)
        nodes = pl.ds(pl.multiple_of(block_col * side, side), side)
        values = jnp.where(live, kept_ref[0, 0, s], 0)
        total_ref[rows, :] += jnp.dot(
            values, panel[nodes, :], preferred_element_type=jnp.float32
        )

    each_slot(lambda s: places[0, 0, s], count_ref[0, 0], slots, send_blocks, work)


def far_kernel(
    values_ref, index_ref, count_ref, second_ref, far_low_ref, far_high_ref, total_ref,
    total_out_ref, theirs_ref, mine_ref, far,
):
    del total_out_ref
    place, core = lax.axis_index("zi"), lax.axis_index("core")
    slots, side = values_ref.shape[2], values_ref.shape[3]
    dests, shard, _ = theirs_ref.shape
    send_blocks = far.shape[0] * STRIDE // side
    half = far_low_ref.shape[0]
    far[:half, :] = far_low_ref[...]
    far[half:, :] = far_high_ref[...]
    per_block = side // shard

    def add_class(shards, group):
        for part in range(per_block):

            def work(s, block_row, block_col, live, part=part):
                node = block_col * per_block + part
                match = live & (lax.rem(node, STRIDE) == group)
                rows = pl.ds(pl.multiple_of(block_row * side, side), side)
                nodes = pl.ds(pl.multiple_of(lax.div(node, STRIDE) * shard, shard), shard)
                values = values_ref[0, 0, s, :, part * shard : (part + 1) * shard]
                total_ref[rows, :] += jnp.dot(
                    jnp.where(match, values, 0),
                    shards[nodes, :],
                    preferred_element_type=jnp.float32,
                )

            @pl.when(lax.rem(group, per_block) == part)
            def _():
                each_slot(
                    lambda s: index_ref[0, 0, s], count_ref[0, 0], slots, send_blocks, work
                )

    add_class(second_ref, lax.rem(place + 1 + 2 * core, STRIDE))
    add_class(far, lax.rem(place + 2, STRIDE))
    for ref, who in ((theirs_ref, 1 - core), (mine_ref, core)):
        for d in range(dests):
            row = pl.multiple_of((2 * d + who) * shard, shard)
            ref[d] = total_ref[pl.ds(row, shard), :].astype(ref.dtype)


def pair_kernel(mine_ref, sibling_ref, out_ref):
    both = mine_ref[...] + sibling_ref[...].astype(jnp.float32)
    out_ref[...] = both.astype(out_ref.dtype)


def final_kernel(parts_ref, weight_ref, bias_ref, out_ref):
    aggregate = jnp.sum(parts_ref[...].astype(jnp.float32), axis=0).astype(jnp.bfloat16)
    mixed = jnp.dot(aggregate, weight_ref[...], preferred_element_type=jnp.float32)
    out_ref[...] = jnp.maximum(mixed + bias_ref[...], 0.0).astype(out_ref.dtype)


def local(features, block_index, block_count, block_values, weight, bias):
    shard, feat = features.shape
    rows = lax.axis_size("zo")
    z_size = rows * STRIDE
    xy_size = lax.axis_size("x") * lax.axis_size("y")

    def turn(array, sign):
        return lax.ppermute(
            array,
            Z + ("core",),
            [
                (2 * z + c, 2 * ((z + sign * (1 - 2 * c)) % z_size) + c)
                for z in range(z_size)
                for c in range(2)
            ],
        )

    own = lax.all_gather(features, "zo", axis=0, tiled=True)
    cut = lax.axis_size("zo") // 2 * shard
    first = [turn(own[:cut], 1), turn(own[cut:], 1)]
    second = turn(own, -1)
    far = [turn(part, 1) for part in first]

    smem = pl.BlockSpec(memory_space=pltpu.SMEM)
    vmem = pl.BlockSpec(memory_space=pltpu.VMEM)
    params = pltpu.CompilerParams(vmem_limit_bytes=VMEM_LIMIT)
    rows_all = 2 * xy_size * shard
    sums = jax.ShapeDtypeStruct((rows_all, feat), jnp.float32)
    half_sums = jax.ShapeDtypeStruct((xy_size, shard, feat), jnp.bfloat16)
    slots, side = block_values.shape[2], block_values.shape[3]

    def cost(share):
        return pl.CostEstimate(
            flops=int(2 * slots * side * side * feat * share),
            bytes_accessed=int(rows_all * feat * 8 * share),
            transcendentals=0,
        )

    tile = (block_values, block_index)
    total, *kept = pl.pallas_call(
        near_kernel,
        out_shape=(
            sums,
            *(jax.ShapeDtypeStruct(a.shape, a.dtype) for a in tile),
        ),
        in_specs=[smem] + [pl.BlockSpec(memory_space=pltpu.HBM)] * 2 + [vmem] * 3,
        out_specs=(vmem, vmem, smem),
        scratch_shapes=[
            pltpu.VMEM((z_size * shard, feat), jnp.bfloat16),
            pltpu.SemaphoreType.DMA,
            pltpu.SemaphoreType.DMA,
        ],
        compiler_params=params,
        cost_estimate=cost(0.5),
    )(
        block_count,
        *(pltpu.with_memory_space_constraint(array, pltpu.HBM) for array in tile),
        own,
        *first,
    )
    _, theirs, mine = pl.pallas_call(
        far_kernel,
        out_shape=(sums, half_sums, jax.ShapeDtypeStruct(half_sums.shape, jnp.float32)),
        in_specs=[vmem, smem, smem] + [vmem] * 4,
        out_specs=(vmem, vmem, vmem),
        input_output_aliases={6: 0},
        scratch_shapes=[pltpu.VMEM(own.shape, own.dtype)],
        compiler_params=params,
        cost_estimate=cost(0.5),
    )(*kept, block_count, second, *far, total)
    sibling = lax.ppermute(theirs, "core", [(0, 1), (1, 0)])
    both = pl.pallas_call(
        pair_kernel,
        out_shape=half_sums,
        in_specs=[vmem] * 2,
        out_specs=vmem,
        compiler_params=params,
    )(mine, sibling)
    parts = lax.all_to_all(both, XY, 0, 0, tiled=True)
    return pl.pallas_call(
        final_kernel,
        out_shape=jax.ShapeDtypeStruct((shard, weight.shape[1]), jnp.bfloat16),
        in_specs=[vmem] * 3,
        out_specs=vmem,
        compiler_params=params,
    )(parts, weight, bias.reshape(1, -1))


def solution(mesh):
    z_size, col = mesh.devices.shape
    side = int(round((col // 2) ** 0.5))
    grid = Mesh(
        mesh.devices.reshape(z_size // STRIDE, STRIDE, side, col // 2 // side, 2),
        Z + XY + ("core",),
    )
    column = XY + ("core",)
    return jax.shard_map(
        local,
        mesh=grid,
        in_specs=(
            P(column + Z, None),
            P(Z, column, None),
            P(Z, column),
            P(Z, column, None, None, None),
            P(),
            P(),
        ),
        out_specs=P(Z + column, None),
        check_vma=False,
    )
```

```python
import jax
import jax.numpy as jnp
from jax import lax
from jax.experimental import pallas as pl
from jax.experimental.pallas import tpu as pltpu
from jax.sharding import Mesh, PartitionSpec as P

STRIDE = 4
Z = ("zo", "zi")
XY = ("x", "y")
VMEM_LIMIT = 16 * 1024 * 1024


def each_slot(places, count, slots, send_blocks, work):
    for s in range(slots):
        e = places(s)
        work(s, lax.div(e, send_blocks), lax.rem(e, send_blocks), s < count)


def near_kernel(
    count_ref, values_ref, index_ref, own_ref, first_low_ref, first_high_ref, second_ref,
    total_ref, kept_ref, places, panel, values_sem, index_sem,
):
    fetches = (
        pltpu.make_async_copy(values_ref, kept_ref, values_sem),
        pltpu.make_async_copy(index_ref, places, index_sem),
    )
    for fetch in fetches:
        fetch.start()
    place, core = lax.axis_index("zi"), lax.axis_index("core")
    slots, side = kept_ref.shape[2], kept_ref.shape[3]
    shard = panel.shape[0] // lax.axis_size("zo") // STRIDE
    classes = lax.axis_size("zo")
    send_blocks = panel.shape[0] // side

    steps = (0, STRIDE - 1 - 2 * core, 1 + 2 * core, 2)
    sources = ((own_ref,), (first_low_ref, first_high_ref), (second_ref,), ())
    for step, refs in zip(steps, sources):
        start = lax.rem(place + step, STRIDE)
        shards = [r[k : k + shard, :] for r in refs for k in range(0, r.shape[0], shard)]
        for k in range(classes):
            rows = pl.ds(pl.multiple_of((start + STRIDE * k) * shard, shard), shard)
            if shards:
                panel[rows, :] = shards[k]
            else:
                panel[rows, :] = jnp.zeros((shard, panel.shape[1]), panel.dtype)
    total_ref[...] = jnp.zeros_like(total_ref)
    for fetch in fetches:
        fetch.wait()

    def work(s, block_row, block_col, live):
        rows = pl.ds(pl.multiple_of(block_row * side, side), side)
        nodes = pl.ds(pl.multiple_of(block_col * side, side), side)
        values = jnp.where(live, kept_ref[0, 0, s], 0)
        total_ref[rows, :] += jnp.dot(
            values, panel[nodes, :], preferred_element_type=jnp.float32
        )

    each_slot(lambda s: places[0, 0, s], count_ref[0, 0], slots, send_blocks, work)


def far_kernel(
    values_ref, index_ref, count_ref, far_low_ref, far_high_ref, total_ref,
    total_out_ref, theirs_ref, mine_ref, far,
):
    del total_out_ref
    place, core = lax.axis_index("zi"), lax.axis_index("core")
    slots, side = values_ref.shape[2], values_ref.shape[3]
    dests, shard, _ = theirs_ref.shape
    send_blocks = far.shape[0] * STRIDE // side
    half = far_low_ref.shape[0]
    far[:half, :] = far_low_ref[...]
    far[half:, :] = far_high_ref[...]
    far_class = lax.rem(place + 2, STRIDE)
    per_block = side // shard

    for part in range(per_block):

        def work(s, block_row, block_col, live, part=part):
            node = block_col * per_block + part
            match = live & (lax.rem(node, STRIDE) == far_class)
            rows = pl.ds(pl.multiple_of(block_row * side, side), side)
            nodes = pl.ds(pl.multiple_of(lax.div(node, STRIDE) * shard, shard), shard)
            values = values_ref[0, 0, s, :, part * shard : (part + 1) * shard]
            total_ref[rows, :] += jnp.dot(
                jnp.where(match, values, 0),
                far[nodes, :],
                preferred_element_type=jnp.float32,
            )

        @pl.when(lax.rem(far_class, per_block) == part)
        def _():
            each_slot(
                lambda s: index_ref[0, 0, s], count_ref[0, 0], slots, send_blocks, work
            )

    for ref, who in ((theirs_ref, 1 - core), (mine_ref, core)):
        for d in range(dests):
            row = pl.multiple_of((2 * d + who) * shard, shard)
            ref[d] = total_ref[pl.ds(row, shard), :].astype(ref.dtype)


def pair_kernel(mine_ref, sibling_ref, out_ref):
    both = mine_ref[...] + sibling_ref[...].astype(jnp.float32)
    out_ref[...] = both.astype(out_ref.dtype)


def final_kernel(parts_ref, weight_ref, bias_ref, out_ref):
    aggregate = jnp.sum(parts_ref[...].astype(jnp.float32), axis=0).astype(jnp.bfloat16)
    mixed = jnp.dot(aggregate, weight_ref[...], preferred_element_type=jnp.float32)
    out_ref[...] = jnp.maximum(mixed + bias_ref[...], 0.0).astype(out_ref.dtype)


def local(features, block_index, block_count, block_values, weight, bias):
    shard, feat = features.shape
    rows = lax.axis_size("zo")
    z_size = rows * STRIDE
    xy_size = lax.axis_size("x") * lax.axis_size("y")

    def turn(array, sign):
        return lax.ppermute(
            array,
            Z + ("core",),
            [
                (2 * z + c, 2 * ((z + sign * (1 - 2 * c)) % z_size) + c)
                for z in range(z_size)
                for c in range(2)
            ],
        )

    own = lax.all_gather(features, "zo", axis=0, tiled=True)
    cut = (lax.axis_size("zo") * 3 // 4) * shard
    first = [turn(own[:cut], 1), turn(own[cut:], 1)]
    second = turn(own, -1)
    far = [turn(part, 1) for part in first]

    smem = pl.BlockSpec(memory_space=pltpu.SMEM)
    vmem = pl.BlockSpec(memory_space=pltpu.VMEM)
    params = pltpu.CompilerParams(vmem_limit_bytes=VMEM_LIMIT)
    rows_all = 2 * xy_size * shard
    sums = jax.ShapeDtypeStruct((rows_all, feat), jnp.float32)
    half_sums = jax.ShapeDtypeStruct((xy_size, shard, feat), jnp.bfloat16)
    slots, side = block_values.shape[2], block_values.shape[3]

    def cost(share):
        return pl.CostEstimate(
            flops=int(2 * slots * side * side * feat * share),
            bytes_accessed=int(rows_all * feat * 8 * share),
            transcendentals=0,
        )

    tile = (block_values, block_index)
    total, *kept = pl.pallas_call(
        near_kernel,
        out_shape=(
            sums,
            *(jax.ShapeDtypeStruct(a.shape, a.dtype) for a in tile),
        ),
        in_specs=[smem] + [pl.BlockSpec(memory_space=pltpu.HBM)] * 2 + [vmem] * 4,
        out_specs=(vmem, vmem, smem),
        scratch_shapes=[
            pltpu.VMEM((z_size * shard, feat), jnp.bfloat16),
            pltpu.SemaphoreType.DMA,
            pltpu.SemaphoreType.DMA,
        ],
        compiler_params=params,
        cost_estimate=cost(0.75),
    )(
        block_count,
        *(pltpu.with_memory_space_constraint(array, pltpu.HBM) for array in tile),
        own,
        *first,
        second,
    )
    _, theirs, mine = pl.pallas_call(
        far_kernel,
        out_shape=(sums, half_sums, jax.ShapeDtypeStruct(half_sums.shape, jnp.float32)),
        in_specs=[vmem, smem, smem] + [vmem] * 3,
        out_specs=(vmem, vmem, vmem),
        input_output_aliases={5: 0},
        scratch_shapes=[pltpu.VMEM(own.shape, own.dtype)],
        compiler_params=params,
        cost_estimate=cost(0.25),
    )(*kept, block_count, *far, total)
    sibling = lax.ppermute(theirs, "core", [(0, 1), (1, 0)])
    both = pl.pallas_call(
        pair_kernel,
        out_shape=half_sums,
        in_specs=[vmem] * 2,
        out_specs=vmem,
        compiler_params=params,
    )(mine, sibling)
    parts = lax.all_to_all(both, XY, 0, 0, tiled=True)
    return pl.pallas_call(
        final_kernel,
        out_shape=jax.ShapeDtypeStruct((shard, weight.shape[1]), jnp.bfloat16),
        in_specs=[vmem] * 3,
        out_specs=vmem,
        compiler_params=params,
    )(parts, weight, bias.reshape(1, -1))


def solution(mesh):
    z_size, col = mesh.devices.shape
    side = int(round((col // 2) ** 0.5))
    grid = Mesh(
        mesh.devices.reshape(z_size // STRIDE, STRIDE, side, col // 2 // side, 2),
        Z + XY + ("core",),
    )
    column = XY + ("core",)
    return jax.shard_map(
        local,
        mesh=grid,
        in_specs=(
            P(column + Z, None),
            P(Z, column, None),
            P(Z, column),
            P(Z, column, None, None, None),
            P(),
            P(),
        ),
        out_specs=P(Z + column, None),
        check_vma=False,
    )
```

```python
import jax
import jax.numpy as jnp
from jax import lax
from jax.experimental import pallas as pl
from jax.experimental.pallas import tpu as pltpu
from jax.sharding import Mesh, PartitionSpec as P

STRIDE = 4
Z = ("zo", "zi")
XY = ("x", "y")
VMEM_LIMIT = 16 * 1024 * 1024


def each_slot(places, count, slots, send_blocks, work):
    for s in range(slots):
        e = places(s)
        work(s, lax.div(e, send_blocks), lax.rem(e, send_blocks), s < count)


def near_kernel(
    count_ref, values_ref, index_ref, own_ref, first_low_ref, first_high_ref, second_ref,
    total_ref, kept_ref, places, panel, values_sem, index_sem,
):
    fetches = (
        pltpu.make_async_copy(values_ref, kept_ref, values_sem),
        pltpu.make_async_copy(index_ref, places, index_sem),
    )
    for fetch in fetches:
        fetch.start()
    place, core = lax.axis_index("zi"), lax.axis_index("core")
    slots, side = kept_ref.shape[2], kept_ref.shape[3]
    shard = panel.shape[0] // lax.axis_size("zo") // STRIDE
    classes = lax.axis_size("zo")
    send_blocks = panel.shape[0] // side

    steps = (0, 1 + 2 * core, STRIDE - 1 - 2 * core, 2)
    sources = ((own_ref,), (first_low_ref, first_high_ref), (second_ref,), ())
    for step, refs in zip(steps, sources):
        start = lax.rem(place + step, STRIDE)
        shards = [r[k : k + shard, :] for r in refs for k in range(0, r.shape[0], shard)]
        for k in range(classes):
            rows = pl.ds(pl.multiple_of((start + STRIDE * k) * shard, shard), shard)
            if shards:
                panel[rows, :] = shards[k]
            else:
                panel[rows, :] = jnp.zeros((shard, panel.shape[1]), panel.dtype)
    total_ref[...] = jnp.zeros_like(total_ref)
    for fetch in fetches:
        fetch.wait()

    def work(s, block_row, block_col, live):
        rows = pl.ds(pl.multiple_of(block_row * side, side), side)
        nodes = pl.ds(pl.multiple_of(block_col * side, side), side)
        values = jnp.where(live, kept_ref[0, 0, s], 0)
        total_ref[rows, :] += jnp.dot(
            values, panel[nodes, :], preferred_element_type=jnp.float32
        )

    each_slot(lambda s: places[0, 0, s], count_ref[0, 0], slots, send_blocks, work)


def far_kernel(
    values_ref, index_ref, count_ref, far_low_ref, far_high_ref, total_ref,
    total_out_ref, theirs_ref, mine_ref, far,
):
    del total_out_ref
    place, core = lax.axis_index("zi"), lax.axis_index("core")
    slots, side = values_ref.shape[2], values_ref.shape[3]
    dests, shard, _ = theirs_ref.shape
    send_blocks = far.shape[0] * STRIDE // side
    half = far_low_ref.shape[0]
    far[:half, :] = far_low_ref[...]
    far[half:, :] = far_high_ref[...]
    far_class = lax.rem(place + 2, STRIDE)
    per_block = side // shard

    for part in range(per_block):

        def work(s, block_row, block_col, live, part=part):
            node = block_col * per_block + part
            match = live & (lax.rem(node, STRIDE) == far_class)
            rows = pl.ds(pl.multiple_of(block_row * side, side), side)
            nodes = pl.ds(pl.multiple_of(lax.div(node, STRIDE) * shard, shard), shard)
            values = values_ref[0, 0, s, :, part * shard : (part + 1) * shard]
            total_ref[rows, :] += jnp.dot(
                jnp.where(match, values, 0),
                far[nodes, :],
                preferred_element_type=jnp.float32,
            )

        @pl.when(lax.rem(far_class, per_block) == part)
        def _():
            each_slot(
                lambda s: index_ref[0, 0, s], count_ref[0, 0], slots, send_blocks, work
            )

    for ref, who in ((theirs_ref, 1 - core), (mine_ref, core)):
        for d in range(dests):
            row = pl.multiple_of((2 * d + who) * shard, shard)
            ref[d] = total_ref[pl.ds(row, shard), :].astype(ref.dtype)


def pair_kernel(mine_ref, sibling_ref, out_ref):
    both = mine_ref[...] + sibling_ref[...].astype(jnp.float32)
    out_ref[...] = both.astype(out_ref.dtype)


def final_kernel(parts_ref, weight_ref, bias_ref, out_ref):
    aggregate = jnp.sum(parts_ref[...].astype(jnp.float32), axis=0).astype(jnp.bfloat16)
    mixed = jnp.dot(aggregate, weight_ref[...], preferred_element_type=jnp.float32)
    out_ref[...] = jnp.maximum(mixed + bias_ref[...], 0.0).astype(out_ref.dtype)


def local(features, block_index, block_count, block_values, weight, bias):
    shard, feat = features.shape
    rows = lax.axis_size("zo")
    z_size = rows * STRIDE
    xy_size = lax.axis_size("x") * lax.axis_size("y")

    def turn(array, sign):
        return lax.ppermute(
            array,
            Z + ("core",),
            [
                (2 * z + c, 2 * ((z + sign * (1 - 2 * c)) % z_size) + c)
                for z in range(z_size)
                for c in range(2)
            ],
        )

    own = lax.all_gather(features, "zo", axis=0, tiled=True)
    cut = (lax.axis_size("zo") * 5 // 8) * shard
    first = [turn(own[:cut], -1), turn(own[cut:], -1)]
    second = turn(own, 1)
    far = [turn(part, -1) for part in first]

    smem = pl.BlockSpec(memory_space=pltpu.SMEM)
    vmem = pl.BlockSpec(memory_space=pltpu.VMEM)
    params = pltpu.CompilerParams(vmem_limit_bytes=VMEM_LIMIT)
    rows_all = 2 * xy_size * shard
    sums = jax.ShapeDtypeStruct((rows_all, feat), jnp.float32)
    half_sums = jax.ShapeDtypeStruct((xy_size, shard, feat), jnp.bfloat16)
    slots, side = block_values.shape[2], block_values.shape[3]

    def cost(share):
        return pl.CostEstimate(
            flops=int(2 * slots * side * side * feat * share),
            bytes_accessed=int(rows_all * feat * 8 * share),
            transcendentals=0,
        )

    tile = (block_values, block_index)
    total, *kept = pl.pallas_call(
        near_kernel,
        out_shape=(
            sums,
            *(jax.ShapeDtypeStruct(a.shape, a.dtype) for a in tile),
        ),
        in_specs=[smem] + [pl.BlockSpec(memory_space=pltpu.HBM)] * 2 + [vmem] * 4,
        out_specs=(vmem, vmem, smem),
        scratch_shapes=[
            pltpu.VMEM((z_size * shard, feat), jnp.bfloat16),
            pltpu.SemaphoreType.DMA,
            pltpu.SemaphoreType.DMA,
        ],
        compiler_params=params,
        cost_estimate=cost(0.75),
    )(
        block_count,
        *(pltpu.with_memory_space_constraint(array, pltpu.HBM) for array in tile),
        own,
        *first,
        second,
    )
    _, theirs, mine = pl.pallas_call(
        far_kernel,
        out_shape=(sums, half_sums, jax.ShapeDtypeStruct(half_sums.shape, jnp.float32)),
        in_specs=[vmem, smem, smem] + [vmem] * 3,
        out_specs=(vmem, vmem, vmem),
        input_output_aliases={5: 0},
        scratch_shapes=[pltpu.VMEM(own.shape, own.dtype)],
        compiler_params=params,
        cost_estimate=cost(0.25),
    )(*kept, block_count, *far, total)
    sibling = lax.ppermute(theirs, "core", [(0, 1), (1, 0)])
    both = pl.pallas_call(
        pair_kernel,
        out_shape=half_sums,
        in_specs=[vmem] * 2,
        out_specs=vmem,
        compiler_params=params,
    )(mine, sibling)
    parts = lax.all_to_all(both, XY, 0, 0, tiled=True)
    return pl.pallas_call(
        final_kernel,
        out_shape=jax.ShapeDtypeStruct((shard, weight.shape[1]), jnp.bfloat16),
        in_specs=[vmem] * 3,
        out_specs=vmem,
        compiler_params=params,
    )(parts, weight, bias.reshape(1, -1))


def solution(mesh):
    z_size, col = mesh.devices.shape
    side = int(round((col // 2) ** 0.5))
    grid = Mesh(
        mesh.devices.reshape(z_size // STRIDE, STRIDE, side, col // 2 // side, 2),
        Z + XY + ("core",),
    )
    column = XY + ("core",)
    return jax.shard_map(
        local,
        mesh=grid,
        in_specs=(
            P(column + Z, None),
            P(Z, column, None),
            P(Z, column),
            P(Z, column, None, None, None),
            P(),
            P(),
        ),
        out_specs=P(Z + column, None),
        check_vma=False,
    )
```
